32 devices in a mesh: groups: 2 (over y), src: 4 (over z), dst: 4 (over x, core).
Axes of the slice: x: 2, y: 2, z: 4, core: 2. Of those that a mesh axis runs over, the one named last changes fastest.
Arguments:
- blocks: bfloat16 [20480, 128, 128], P(('groups', 'src', 'dst')), parts along dimension 0, may hold values from -1 to 1
- block_rows: int32 [20480], P(('groups', 'src', 'dst')), parts along dimension 0, may hold values from 0 to 255, as said below
- block_cols: int32 [20480], P(('groups', 'src', 'dst')), parts along dimension 0, may hold values from 0 to 127, as said below
- row_counts: int32 [65536], P(('groups', 'src')), parts along dimension 0, may hold values from 16 to 5952
- col_counts: int32 [32768], P(('groups', 'dst')), parts along dimension 0, may hold values from 16 to 5952
- start_panel: float32 [32, 32768], P(None, ('groups', 'dst')), parts along dimension 1, may hold values from -30 to 30
Outputs:
- coherent_panel: float32 [32, 32768], P(None, ('groups', 'dst')), parts along dimension 1
The draws below stay inside these ranges and needn't reach their ends.
There are 2 independent parts, one for each index of `groups`. The reference program is written for one: setup_inputs(seed, part) draws one part's arguments, and reference() takes and returns one part's arrays. A program takes and returns all parts, laid end to end along the dimension named above; each array names one. Nothing has to cross between parts.
Inputs may be any that keep to these rules, and one draw needn't show every extreme that they name: `block_rows`: with q = j // 640, s = q // n and d = q % n (n devices along dst), entry j lies in block rows 64 * s to 64 * s + 63; every block row is named by exactly 40 entries, no two of them with the same block column. `block_cols`: with s and d as for block_rows, entry j lies in block columns 32 * d to 32 * d + 31; every block column is named by some entry.
All inputs are finite; a program needn't handle non-finite values.
Results may differ from the reference program's by a relative error of at most 0.0047.
Values may be sent and summed in bfloat16 or wider, within the bound.
A program may use at most 128 MiB of HBM per device.

```python
import math
import jax
import jax.numpy as jnp
from jax import lax

BOX = 128
PANEL = 32
BPR = 40
ITERS = 2
RBS = 64
CBD = 32
BLK_DEV = 640
NBLK = 10240
NSRC = 32768
NDST = 16384
N_SRC = 4
N_DST = 4


def count_draw(key, count_total):
    mant_key = jax.random.fold_in(key, 5)
    expo_key = jax.random.fold_in(key, 6)
    mantissa = jax.random.randint(mant_key, (count_total,), 16, 32)
    exponent = jax.random.randint(expo_key, (count_total,), 0, 7)
    places = jnp.arange(count_total, dtype=jnp.int32)
    tilted = 192 - 128 * places // count_total
    values = jnp.left_shift(mantissa, exponent) * tilted // 64
    values = jnp.where(places == 0, 5952, values)
    values = jnp.where(places == count_total - 1, 16, values)
    return values.astype(jnp.int32)


def draw_row_counts(key, part):
    return count_draw(jax.random.fold_in(key, 21), NSRC)


def draw_col_counts(key, part):
    return count_draw(jax.random.fold_in(key, 22), NDST)


def block_layout(key):
    rows_key = jax.random.fold_in(key, 31)
    cols_key = jax.random.fold_in(key, 32)
    order_key = jax.random.fold_in(key, 33)
    shifts = jax.vmap(lambda one_key: jax.random.permutation(one_key, RBS))(jax.random.split(rows_key, N_SRC)) % N_DST
    dst_ids = jnp.arange(N_DST, dtype=jnp.int32)
    residue = (dst_ids[None, :, None] - shifts[:, None, :]) % N_DST
    per_row = (BPR - residue + N_DST - 1) // N_DST
    row_ends = jnp.cumsum(per_row, axis=-1).reshape(N_SRC * N_DST, RBS)
    slots = jnp.arange(BLK_DEV, dtype=jnp.int32)
    local_row = jax.vmap(lambda ends: jnp.searchsorted(ends, slots, side='right'))(row_ends).astype(jnp.int32)
    col_perm = jax.vmap(lambda one_key: jax.random.permutation(one_key, CBD))(jax.random.split(cols_key, N_SRC * N_DST))
    local_col = jnp.take(col_perm, slots % CBD, axis=1).astype(jnp.int32)
    orders = jax.vmap(lambda one_key: jax.random.permutation(one_key, BLK_DEV))(jax.random.split(order_key, N_SRC * N_DST))
    local_row = jnp.take_along_axis(local_row, orders, axis=1).reshape(N_SRC, N_DST, BLK_DEV)
    local_col = jnp.take_along_axis(local_col, orders, axis=1).reshape(N_SRC, N_DST, BLK_DEV)
    global_row = local_row + RBS * jnp.arange(N_SRC, dtype=jnp.int32)[:, None, None]
    global_col = local_col + CBD * jnp.arange(N_DST, dtype=jnp.int32)[None, :, None]
    return (global_row.reshape(-1).astype(jnp.int32), global_col.reshape(-1).astype(jnp.int32))


def draw_block_rows(key, part):
    return block_layout(key)[0]


def draw_block_cols(key, part):
    return block_layout(key)[1]


def draw_start_panel(key, part):
    scale_key = jax.random.fold_in(key, 41)
    noise_key = jax.random.fold_in(key, 43)
    column_scale = jnp.exp(jax.random.uniform(scale_key, (PANEL, 1), minval=0.0, maxval=math.log(10.0)))
    values = column_scale * jax.random.truncated_normal(noise_key, -3.0, 3.0, (PANEL, NDST))
    return values.astype(jnp.float32)


def block_scale(key, extent, cuts, least, top_value):
    def one(position, blocks):
        heights = jax.random.uniform(jax.random.fold_in(jax.random.fold_in(key, 6), position), (blocks,), jnp.float32, least / len(cuts), top_value / len(cuts))
        return jnp.repeat(jnp.exp(heights), extent[position] // blocks).reshape((-1,) + (1,) * (len(extent) - position - 1))

    factor_of = one(*cuts[0])
    for cut in cuts[1:]:
        factor_of = factor_of * one(*cut)
    return factor_of


def setup_inputs(seed: int = 0, part: int = 0) -> dict:
    streams_of = jax.random.split(jax.random.key(seed), 7)
    part_splits = jax.random.split(jax.random.fold_in(streams_of[6], part), 7)
    blocks = jnp.clip(jax.random.uniform(part_splits[0], (NBLK, BOX, BOX), jnp.float32, -1.0, 1.0) * block_scale(part_splits[0], (NBLK, BOX, BOX), ((0, 16),), -0.4, 0.0), -1.0, 1.0).astype(jnp.bfloat16)
    block_rows = draw_block_rows(jax.random.fold_in(jax.random.fold_in(streams_of[6], part), 71), part)
    block_cols = draw_block_cols(jax.random.fold_in(jax.random.fold_in(streams_of[6], part), 71), part)
    row_counts = draw_row_counts(jax.random.fold_in(jax.random.fold_in(streams_of[6], part), 71), part)
    col_counts = draw_col_counts(jax.random.fold_in(jax.random.fold_in(streams_of[6], part), 71), part)
    start_panel = draw_start_panel(jax.random.fold_in(jax.random.fold_in(streams_of[6], part), 71), part)
    return {"blocks": blocks, "block_rows": block_rows, "block_cols": block_cols, "row_counts": row_counts, "col_counts": col_counts, "start_panel": start_panel}


def orthonormal(panel_in):
    gram_matrix = jnp.einsum('ckb,clb->kl', panel_in, panel_in, precision=lax.Precision.HIGHEST) / NDST
    factor = jnp.linalg.cholesky(gram_matrix)
    inverse = jax.scipy.linalg.solve_triangular(factor, jnp.eye(PANEL, dtype=jnp.float32), lower=True)
    return jnp.einsum('kl,clb->ckb', inverse, panel_in, precision=lax.Precision.HIGHEST)

def reference(blocks, block_rows, block_cols, row_counts, col_counts, start_panel):
    row_blocks = NSRC // BOX
    col_blocks = NDST // BOX
    step_count = NBLK // BLK_DEV
    row_scale = row_counts.astype(jnp.float32).reshape(row_blocks, 1, BOX)
    col_scale = jnp.sqrt(col_counts.astype(jnp.float32)).reshape(col_blocks, 1, BOX)
    tile_sets = blocks.reshape(step_count, BLK_DEV, BOX, BOX)
    row_sets = block_rows.reshape(step_count, BLK_DEV)
    col_sets = block_cols.reshape(step_count, BLK_DEV)
    current = start_panel.reshape(PANEL, col_blocks, BOX).transpose(1, 0, 2)
    for sweep_index in range(ITERS):
        scaled = (current / col_scale).astype(jnp.bfloat16)

        def forward_step(running, entries):
            tile_group, row_ids, col_ids = entries
            picked = scaled[col_ids].astype(jnp.float32)
            contrib = jnp.einsum('bkj,bij->bki', picked, tile_group.astype(jnp.float32), precision=lax.Precision.HIGHEST)
            return (running.at[row_ids].add(contrib), None)
        product_rows, _ = lax.scan(forward_step, jnp.zeros((row_blocks, PANEL, BOX), jnp.float32), (tile_sets, row_sets, col_sets))
        weighted = (product_rows / row_scale).astype(jnp.bfloat16)

        def adjoint_step(running, entries):
            tile_group, row_ids, col_ids = entries
            picked = weighted[row_ids].astype(jnp.float32)
            contrib = jnp.einsum('bki,bij->bkj', picked, tile_group.astype(jnp.float32), precision=lax.Precision.HIGHEST)
            return (running.at[col_ids].add(contrib), None)
        product_cols, _ = lax.scan(adjoint_step, jnp.zeros((col_blocks, PANEL, BOX), jnp.float32), (tile_sets, row_sets, col_sets))
        current = orthonormal(orthonormal(product_cols / col_scale))
    return current.transpose(1, 0, 2).reshape(PANEL, NDST)
```

```python
import functools

import jax
import jax.numpy as jnp
from jax import lax
from jax.experimental import pallas as pl
from jax.experimental.pallas import tpu as pltpu
from jax.sharding import PartitionSpec as P

ITERS = 2
UNROLL = 8
VMEM = pl.BlockSpec(memory_space=pltpu.VMEM)
SMEM = pl.BlockSpec(memory_space=pltpu.SMEM)
LIMIT = 48 * 1024 * 1024


def lanes(index, side):
    return pl.ds(pl.multiple_of(index * side, side), side)


def sweep_kernel(contract, gather_ref, scatter_ref, panel_ref, scale_ref, blocks_ref, out_ref, scaled):
    side = blocks_ref.shape[1]
    count = blocks_ref.shape[0]
    step = pl.program_id(0)

    @pl.when(step == 0)
    def _():
        scaled[...] = (panel_ref[...] / scale_ref[...]).astype(jnp.bfloat16)
        out_ref[...] = jnp.zeros_like(out_ref)

    @pl.loop(0, count // UNROLL)
    def _(chunk):
        terms = []
        for k in range(UNROLL):
            b = chunk * UNROLL + k
            g = gather_ref[step * count + b]
            terms.append(
                lax.dot_general(
                    scaled[:, lanes(g, side)],
                    blocks_ref[b],
                    (((1,), (contract,)), ((), ())),
                    preferred_element_type=jnp.float32,
                )
            )
        for k in range(UNROLL):
            s = scatter_ref[step * count + chunk * UNROLL + k]
            out_ref[:, lanes(s, side)] += terms[k]


def sweep(contract, gather_ids, scatter_ids, panel, scale, blocks, out_width):
    total, side, _ = blocks.shape
    count = 32 if total % 32 == 0 else UNROLL
    width = panel.shape[0]
    return pl.pallas_call(
        functools.partial(sweep_kernel, contract),
        grid=(total // count,),
        in_specs=[
            SMEM,
            SMEM,
            pl.BlockSpec(panel.shape, lambda i: (0, 0)),
            pl.BlockSpec(scale.shape, lambda i: (0, 0)),
            pl.BlockSpec((count, side, side), lambda i: (i, 0, 0)),
        ],
        out_specs=pl.BlockSpec((width, out_width), lambda i: (0, 0)),
        out_shape=jax.ShapeDtypeStruct((width, out_width), jnp.float32),
        scratch_shapes=[pltpu.VMEM(panel.shape, jnp.bfloat16)],
        compiler_params=pltpu.CompilerParams(vmem_limit_bytes=LIMIT),
    )(gather_ids, scatter_ids, panel, scale, blocks)


def gram(panel):
    return lax.dot_general(
        panel,
        panel,
        (((1,), (1,)), ((), ())),
        precision=lax.Precision.HIGHEST,
        preferred_element_type=jnp.float32,
    )


def inverse_factor(matrix):
    n = matrix.shape[0]
    row = lax.broadcasted_iota(jnp.int32, (n, n), 0)
    col = lax.broadcasted_iota(jnp.int32, (n, n), 1)
    both = jnp.concatenate([matrix, (row == col).astype(jnp.float32)], axis=1)
    row = lax.broadcasted_iota(jnp.int32, (n, 1), 0)
    for j in range(n):
        root = jnp.sqrt(both[j : j + 1, j : j + 1])
        pivot = both[j : j + 1, :] / root
        factor = both[:, j : j + 1] / root
        both = jnp.where(row == j, pivot, both - jnp.where(row > j, factor, 0.0) * pivot)
    return both[:, n:]


def apply(inverse, panel):
    return jnp.dot(
        inverse, panel, precision=lax.Precision.HIGHEST, preferred_element_type=jnp.float32
    )


def scale_gram_kernel(sums_ref, scale_ref, out_ref, gram_ref):
    out_ref[...] = sums_ref[...] / scale_ref[...]
    gram_ref[...] = gram(out_ref[...])


def apply_gram_kernel(box_total, gram_in_ref, panel_ref, out_ref, gram_ref):
    out_ref[...] = apply(inverse_factor(gram_in_ref[...] / box_total), panel_ref[...])
    gram_ref[...] = gram(out_ref[...])


def apply_kernel(box_total, gram_in_ref, panel_ref, out_ref):
    out_ref[...] = apply(inverse_factor(gram_in_ref[...] / box_total), panel_ref[...])


def small(kernel, outs, *args):
    return pl.pallas_call(
        kernel,
        in_specs=[VMEM] * len(args),
        out_specs=jax.tree.map(lambda _: VMEM, outs),
        out_shape=outs,
        compiler_params=pltpu.CompilerParams(vmem_limit_bytes=LIMIT),
    )(*args)


def per_device(blocks, block_rows, block_cols, row_counts, col_counts, start_panel):
    side = blocks.shape[1]
    width = start_panel.shape[0]
    rows = row_counts.shape[0]
    cols = col_counts.shape[0]
    box_total = float(cols * lax.axis_size("dst"))
    local_rows = block_rows - lax.axis_index("src") * (rows // side)
    local_cols = block_cols - lax.axis_index("dst") * (cols // side)
    row_scale = row_counts.astype(jnp.float32).reshape(1, rows)
    col_scale = jnp.sqrt(col_counts.astype(jnp.float32)).reshape(1, cols)
    panel = start_panel
    panel_type = jax.ShapeDtypeStruct((width, cols), jnp.float32)
    gram_type = jax.ShapeDtypeStruct((width, width), jnp.float32)
    for _ in range(ITERS):
        u = sweep(1, local_cols, local_rows, panel, col_scale, blocks, rows)
        u = lax.psum(u, "dst")
        w = sweep(0, local_rows, local_cols, u, row_scale, blocks, cols)
        w = lax.psum(w, "src")
        w, g = small(scale_gram_kernel, (panel_type, gram_type), w, col_scale)
        g = lax.psum(g, "dst")
        q, g = small(
            functools.partial(apply_gram_kernel, box_total), (panel_type, gram_type), g, w
        )
        g = lax.psum(g, "dst")
        panel = small(functools.partial(apply_kernel, box_total), panel_type, g, q)
    return panel


def solution(mesh):
    return jax.shard_map(
        per_device,
        mesh=mesh,
        in_specs=(
            P(("groups", "src", "dst"), None, None),
            P(("groups", "src", "dst")),
            P(("groups", "src", "dst")),
            P(("groups", "src")),
            P(("groups", "dst")),
            P(None, ("groups", "dst")),
        ),
        out_specs=P(None, ("groups", "dst")),
        check_vma=False,
    )
```

```python
import functools

import jax
import jax.numpy as jnp
from jax import lax
from jax.experimental import pallas as pl
from jax.experimental.pallas import tpu as pltpu
from jax.sharding import PartitionSpec as P

ITERS = 2
UNROLL = 8
MESH = pl.DeviceIdType.MESH
VMEM = pl.BlockSpec(memory_space=pltpu.VMEM)
SMEM = pl.BlockSpec(memory_space=pltpu.SMEM)
LIMIT = 48 * 1024 * 1024


def lanes(index, side):
    return pl.ds(pl.multiple_of(index * side, side), side)


def sweep_kernel(contract, gather_ref, scatter_ref, *refs):
    if len(refs) == 5:
        panel_ref, scale_ref, blocks_ref, out_ref, scaled = refs
    else:
        scaled, blocks_ref, out_ref = refs
    side = blocks_ref.shape[1]
    count = blocks_ref.shape[0]
    step = pl.program_id(0)

    @pl.when(step == 0)
    def _():
        if len(refs) == 5:
            scaled[...] = (panel_ref[...] / scale_ref[...]).astype(jnp.bfloat16)
        out_ref[...] = jnp.zeros_like(out_ref)

    @pl.loop(0, count // UNROLL)
    def _(chunk):
        terms = []
        for k in range(UNROLL):
            b = chunk * UNROLL + k
            g = gather_ref[step * count + b]
            terms.append(
                lax.dot_general(
                    scaled[:, lanes(g, side)],
                    blocks_ref[b],
                    (((1,), (contract,)), ((), ())),
                    preferred_element_type=jnp.float32,
                )
            )
        for k in range(UNROLL):
            s = scatter_ref[step * count + chunk * UNROLL + k]
            out_ref[:, lanes(s, side)] += terms[k]


def sweep(contract, gather_ids, scatter_ids, panel, scale, blocks, out_width):
    total, side, _ = blocks.shape
    count = 32 if total % 32 == 0 else UNROLL
    width = panel.shape[0]
    small = [panel] if scale is None else [panel, scale]
    return pl.pallas_call(
        functools.partial(sweep_kernel, contract),
        grid=(total // count,),
        in_specs=[
            SMEM,
            SMEM,
            *(pl.BlockSpec(a.shape, lambda i: (0, 0)) for a in small),
            pl.BlockSpec((count, side, side), lambda i: (i, 0, 0)),
        ],
        out_specs=pl.BlockSpec((width, out_width), lambda i: (0, 0)),
        out_shape=jax.ShapeDtypeStruct((width, out_width), jnp.float32),
        scratch_shapes=[pltpu.VMEM(panel.shape, jnp.bfloat16)] * (scale is not None),
        compiler_params=pltpu.CompilerParams(vmem_limit_bytes=LIMIT),
    )(gather_ids, scatter_ids, *small, blocks)


def gram(panel):
    return lax.dot_general(
        panel,
        panel,
        (((1,), (1,)), ((), ())),
        precision=lax.Precision.HIGHEST,
        preferred_element_type=jnp.float32,
    )


def inverse_factor(matrix):
    n = matrix.shape[0]
    row = lax.broadcasted_iota(jnp.int32, (n, n), 0)
    col = lax.broadcasted_iota(jnp.int32, (n, n), 1)
    both = jnp.concatenate([matrix, (row == col).astype(jnp.float32)], axis=1)
    row = lax.broadcasted_iota(jnp.int32, (n, 1), 0)
    for j in range(n):
        root = jnp.sqrt(both[j : j + 1, j : j + 1])
        pivot = both[j : j + 1, :] / root
        factor = both[:, j : j + 1] / root
        both = jnp.where(row == j, pivot, both - jnp.where(row > j, factor, 0.0) * pivot)
    return both[:, n:]


def apply(inverse, panel):
    return jnp.dot(
        inverse, panel, precision=lax.Precision.HIGHEST, preferred_element_type=jnp.float32
    )


def greet(axes):
    barrier = pltpu.get_barrier_semaphore()
    number = 0
    for axis in axes:
        n = lax.axis_size(axis)
        me = lax.axis_index(axis)
        for k in range(1, n):
            pl.semaphore_signal(
                barrier, inc=1, device_id={axis: lax.rem(me + k, n)}, device_id_type=MESH
            )
            number += 1
    pl.semaphore_wait(barrier, number)


def scatter_sums(axis, sums_ref, half, landing, sems):
    n = lax.axis_size(axis)
    me = lax.axis_index(axis)
    part = sums_ref.shape[1] // n
    copies = []
    for k in range(1, n):
        peer = lax.rem(me + k, n)
        copy = pltpu.make_async_remote_copy(
            src_ref=half.at[:, lanes(peer, part)],
            dst_ref=landing.at[k],
            send_sem=sems.at[0, k],
            recv_sem=sems.at[1, k],
            device_id={axis: peer},
            device_id_type=MESH,
        )
        copy.start()
        copies.append(copy)
    mine = lanes(me, part)
    total = sums_ref[:, mine]
    for k in range(1, n):
        copies[k - 1].wait_recv()
        total = total + landing[k].astype(jnp.float32)
    return total, mine, copies


def gather_start(axis, whole, mine, sems):
    n = lax.axis_size(axis)
    me = lax.axis_index(axis)
    copies = []
    for k in range(1, n):
        copy = pltpu.make_async_remote_copy(
            src_ref=whole.at[:, mine],
            dst_ref=whole.at[:, mine],
            send_sem=sems.at[0, k],
            recv_sem=sems.at[1, k],
            device_id={axis: lax.rem(me + k, n)},
            device_id_type=MESH,
        )
        copy.start()
        copies.append(copy)
    return copies


def sum_small(axis, value, slots, sems):
    n = lax.axis_size(axis)
    me = lax.axis_index(axis)
    slots[me] = value
    copies = []
    for k in range(1, n):
        copy = pltpu.make_async_remote_copy(
            src_ref=slots.at[me],
            dst_ref=slots.at[me],
            send_sem=sems.at[0, k],
            recv_sem=sems.at[1, k],
            device_id={axis: lax.rem(me + k, n)},
            device_id_type=MESH,
        )
        copy.start()
        copies.append(copy)
    for copy in copies:
        copy.wait()
    total = slots[0]
    for k in range(1, n):
        total = total + slots[k]
    return total


def rows_kernel(axis, sums_ref, scale_ref, out_ref, half, landing, whole, scatter_sems, gather_sems):
    half[...] = sums_ref[...].astype(jnp.bfloat16)
    greet((axis,))
    total, mine, sent = scatter_sums(axis, sums_ref, half, landing, scatter_sems)
    whole[:, mine] = (total / scale_ref[:, mine]).astype(jnp.bfloat16)
    gathered = gather_start(axis, whole, mine, gather_sems)
    for copy in sent:
        copy.wait_send()
    for copy in gathered:
        copy.wait()
    out_ref[...] = whole[...]


def panel_kernel(
    box_total,
    sums_ref,
    scale_ref,
    out_ref,
    half,
    landing,
    whole,
    slots_src,
    slots_dst,
    slots_second,
    scatter_sems,
    gather_sems,
    src_sems,
    dst_sems,
    second_sems,
):
    half[...] = sums_ref[...].astype(jnp.bfloat16)
    greet(("src", "dst"))
    total, mine, sent = scatter_sums("src", sums_ref, half, landing, scatter_sems)
    own = total / scale_ref[:, mine]
    whole[:, mine] = own
    gathered = gather_start("src", whole, mine, gather_sems)
    first = sum_small("src", gram(own), slots_src, src_sems)
    first = sum_small("dst", first, slots_dst, dst_sems)
    inverse = inverse_factor(first / box_total)
    for copy in sent:
        copy.wait_send()
    for copy in gathered:
        copy.wait()
    out_ref[...] = apply(inverse, whole[...])
    second = sum_small("dst", gram(out_ref[...]), slots_second, second_sems)
    out_ref[...] = apply(inverse_factor(second / box_total), out_ref[...])


def sem_pairs(n):
    return pltpu.SemaphoreType.DMA((2, n))


def reduce_rows(sums, scale):
    n = lax.axis_size("dst")
    width, extent = sums.shape
    return pl.pallas_call(
        functools.partial(rows_kernel, "dst"),
        in_specs=[VMEM] * 2,
        out_specs=VMEM,
        out_shape=jax.ShapeDtypeStruct(sums.shape, jnp.bfloat16),
        scratch_shapes=[
            pltpu.VMEM(sums.shape, jnp.bfloat16),
            pltpu.VMEM((n, width, extent // n), jnp.bfloat16),
            pltpu.VMEM(sums.shape, jnp.bfloat16),
            sem_pairs(n),
            sem_pairs(n),
        ],
        compiler_params=pltpu.CompilerParams(
            collective_id=0, has_side_effects=True, vmem_limit_bytes=LIMIT
        ),
    )(sums, scale)


def reduce_panel(sums, scale, box_total):
    n_src = lax.axis_size("src")
    n_dst = lax.axis_size("dst")
    width, extent = sums.shape
    return pl.pallas_call(
        functools.partial(panel_kernel, box_total),
        in_specs=[VMEM] * 2,
        out_specs=VMEM,
        out_shape=jax.ShapeDtypeStruct(sums.shape, jnp.float32),
        scratch_shapes=[
            pltpu.VMEM(sums.shape, jnp.bfloat16),
            pltpu.VMEM((n_src, width, extent // n_src), jnp.bfloat16),
            pltpu.VMEM(sums.shape, jnp.float32),
            pltpu.VMEM((n_src, width, width), jnp.float32),
            pltpu.VMEM((n_dst, width, width), jnp.float32),
            pltpu.VMEM((n_dst, width, width), jnp.float32),
            sem_pairs(n_src),
            sem_pairs(n_src),
            sem_pairs(n_src),
            sem_pairs(n_dst),
            sem_pairs(n_dst),
        ],
        compiler_params=pltpu.CompilerParams(
            collective_id=1, has_side_effects=True, vmem_limit_bytes=LIMIT
        ),
    )(sums, scale)


def per_device(blocks, block_rows, block_cols, row_counts, col_counts, start_panel):
    side = blocks.shape[1]
    width = start_panel.shape[0]
    rows = row_counts.shape[0]
    cols = col_counts.shape[0]
    box_total = float(cols * lax.axis_size("dst"))
    local_rows = block_rows - lax.axis_index("src") * (rows // side)
    local_cols = block_cols - lax.axis_index("dst") * (cols // side)
    row_scale = row_counts.astype(jnp.float32).reshape(1, rows)
    col_scale = jnp.sqrt(col_counts.astype(jnp.float32)).reshape(1, cols)
    panel = start_panel
    for _ in range(ITERS):
        u = sweep(1, local_cols, local_rows, panel, col_scale, blocks, rows)
        z = reduce_rows(u, row_scale)
        w = sweep(0, local_rows, local_cols, z, None, blocks, cols)
        panel = reduce_panel(w, col_scale, box_total)
    return panel


def solution(mesh):
    return jax.shard_map(
        per_device,
        mesh=mesh,
        in_specs=(
            P(("groups", "src", "dst"), None, None),
            P(("groups", "src", "dst")),
            P(("groups", "src", "dst")),
            P(("groups", "src")),
            P(("groups", "dst")),
            P(None, ("groups", "dst")),
        ),
        out_specs=P(None, ("groups", "dst")),
        check_vma=False,
    )
```

```python
import functools

import jax
import jax.numpy as jnp
from jax import lax
from jax.experimental import pallas as pl
from jax.experimental.pallas import tpu as pltpu
from jax.sharding import PartitionSpec as P

ITERS = 2
CHUNKS = (128, 64, 32, 16, 8)
MESH = pl.DeviceIdType.MESH
VMEM = pl.BlockSpec(memory_space=pltpu.VMEM)
SMEM = pl.BlockSpec(memory_space=pltpu.SMEM)
LIMIT = 48 * 1024 * 1024


def lanes(index, side):
    return pl.ds(pl.multiple_of(index * side, side), side)


def root_of(counts):
    return jnp.sqrt(counts.astype(jnp.float32))


def sweep_kernel(contract, unroll, gather_ref, scatter_ref, *refs):
    if len(refs) == 5:
        panel_ref, scale_ref, blocks_ref, out_ref, scaled = refs
    else:
        scaled, blocks_ref, out_ref = refs
    side = blocks_ref.shape[1]
    count = blocks_ref.shape[0]
    step = pl.program_id(0)

    @pl.when(step == 0)
    def _():
        if len(refs) == 5:
            scaled[...] = (panel_ref[...] / root_of(scale_ref[...])).astype(jnp.bfloat16)
        out_ref[...] = jnp.zeros_like(out_ref)

    @pl.loop(0, count // unroll)
    def _(chunk):
        terms = []
        for k in range(unroll):
            b = chunk * unroll + k
            g = lax.rem(gather_ref[step * count + b], scaled.shape[1] // side)
            terms.append(
                lax.dot_general(
                    scaled[:, lanes(g, side)],
                    blocks_ref[b],
                    (((1,), (contract,)), ((), ())),
                    preferred_element_type=jnp.float32,
                )
            )
        for k in range(unroll):
            s = lax.rem(scatter_ref[step * count + chunk * unroll + k], out_ref.shape[1] // side)
            out_ref[:, lanes(s, side)] += terms[k]


def sweep(contract, gather_ids, scatter_ids, panel, scale, blocks, out_width):
    total, side, _ = blocks.shape
    count = next(c for c in (*CHUNKS, 1) if total % c == 0)
    unroll = min(count, 64)
    width = panel.shape[0]
    small = [panel] if scale is None else [panel, scale]
    return pl.pallas_call(
        functools.partial(sweep_kernel, contract, unroll),
        grid=(total // count,),
        in_specs=[
            SMEM,
            SMEM,
            *(pl.BlockSpec(a.shape, lambda i: (0, 0)) for a in small),
            pl.BlockSpec((count, side, side), lambda i: (i, 0, 0)),
        ],
        out_specs=pl.BlockSpec((width, out_width), lambda i: (0, 0)),
        out_shape=jax.ShapeDtypeStruct((width, out_width), jnp.float32),
        scratch_shapes=[pltpu.VMEM(panel.shape, jnp.bfloat16)] * (scale is not None),
        compiler_params=pltpu.CompilerParams(vmem_limit_bytes=LIMIT),
    )(gather_ids, scatter_ids, *small, blocks)


def gram(panel):
    return lax.dot_general(
        panel,
        panel,
        (((1,), (1,)), ((), ())),
        precision=lax.Precision.HIGHEST,
        preferred_element_type=jnp.float32,
    )


def inverse_factor(matrix):
    n = matrix.shape[0]
    row = lax.broadcasted_iota(jnp.int32, (n, n), 0)
    col = lax.broadcasted_iota(jnp.int32, (n, n), 1)
    diagonal = row == col
    both = jnp.concatenate([matrix, diagonal.astype(jnp.float32)], axis=1)
    row = lax.broadcasted_iota(jnp.int32, both.shape, 0)
    for j in range(n - 1):
        factor = jnp.broadcast_to(both[:, j : j + 1], both.shape)
        pivot = both[j : j + 1, :] / factor[j : j + 1, :]
        both = both - jnp.where(row > j, factor, 0.0) * pivot
    pivots = jnp.sum(jnp.where(diagonal, both[:, :n], 0.0), axis=1, keepdims=True)
    return both[:, n:] / jnp.sqrt(pivots)


def apply(inverse, panel):
    return jnp.dot(
        inverse, panel, precision=lax.Precision.HIGHEST, preferred_element_type=jnp.float32
    )


def greet(axes):
    barrier = pltpu.get_barrier_semaphore()
    number = 0
    for axis in axes:
        n = lax.axis_size(axis)
        me = lax.axis_index(axis)
        for k in range(1, n):
            pl.semaphore_signal(
                barrier, inc=1, device_id={axis: lax.rem(me + k, n)}, device_id_type=MESH
            )
            number += 1
    pl.semaphore_wait(barrier, number)


def scatter_sums(axis, sums_ref, half, landing, sems):
    n = lax.axis_size(axis)
    me = lax.axis_index(axis)
    part = sums_ref.shape[1] // n
    copies = []
    for k in range(1, n):
        peer = lax.rem(me + k, n)
        copy = pltpu.make_async_remote_copy(
            src_ref=half.at[:, lanes(peer, part)],
            dst_ref=landing.at[k],
            send_sem=sems.at[0, k],
            recv_sem=sems.at[1, k],
            device_id={axis: peer},
            device_id_type=MESH,
        )
        copy.start()
        copies.append(copy)
    mine = lanes(me, part)
    total = sums_ref[:, mine]
    for k in range(1, n):
        copies[k - 1].wait_recv()
        total = total + landing[k].astype(jnp.float32)
    return total, mine, copies


def gather_start(axis, whole, mine, sems):
    n = lax.axis_size(axis)
    me = lax.axis_index(axis)
    copies = []
    for k in range(1, n):
        copy = pltpu.make_async_remote_copy(
            src_ref=whole.at[:, mine],
            dst_ref=whole.at[:, mine],
            send_sem=sems.at[0, k],
            recv_sem=sems.at[1, k],
            device_id={axis: lax.rem(me + k, n)},
            device_id_type=MESH,
        )
        copy.start()
        copies.append(copy)
    return copies


def sum_small(axis, value, slots, sems):
    n = lax.axis_size(axis)
    me = lax.axis_index(axis)
    slots[me] = value
    copies = []
    for k in range(1, n):
        copy = pltpu.make_async_remote_copy(
            src_ref=slots.at[me],
            dst_ref=slots.at[me],
            send_sem=sems.at[0, k],
            recv_sem=sems.at[1, k],
            device_id={axis: lax.rem(me + k, n)},
            device_id_type=MESH,
        )
        copy.start()
        copies.append(copy)
    for copy in copies:
        copy.wait()
    total = slots[0]
    for k in range(1, n):
        total = total + slots[k]
    return total


def rows_kernel(axis, sums_ref, scale_ref, out_ref, half, landing, whole, scatter_sems, gather_sems):
    half[...] = sums_ref[...].astype(jnp.bfloat16)
    greet((axis,))
    total, mine, sent = scatter_sums(axis, sums_ref, half, landing, scatter_sems)
    whole[:, mine] = (total / scale_ref[:, mine].astype(jnp.float32)).astype(jnp.bfloat16)
    gathered = gather_start(axis, whole, mine, gather_sems)
    for copy in sent:
        copy.wait_send()
    for copy in gathered:
        copy.wait()
    out_ref[...] = whole[...]


def panel_kernel(
    box_total,
    sums_ref,
    scale_ref,
    out_ref,
    half,
    landing,
    whole,
    slots_src,
    slots_dst,
    slots_second,
    scatter_sems,
    gather_sems,
    src_sems,
    dst_sems,
    second_sems,
):
    half[...] = sums_ref[...].astype(jnp.bfloat16)
    greet(("src", "dst"))
    total, mine, sent = scatter_sums("src", sums_ref, half, landing, scatter_sems)
    own = total / root_of(scale_ref[:, mine])
    whole[:, mine] = own
    gathered = gather_start("src", whole, mine, gather_sems)
    first = sum_small("src", gram(own), slots_src, src_sems)
    first = sum_small("dst", first, slots_dst, dst_sems)
    inverse = inverse_factor(first / box_total)
    for copy in sent:
        copy.wait_send()
    for copy in gathered:
        copy.wait()
    out_ref[...] = apply(inverse, whole[...])
    second = sum_small("dst", gram(out_ref[...]), slots_second, second_sems)
    out_ref[...] = apply(inverse_factor(second / box_total), out_ref[...])


def sem_pairs(n):
    return pltpu.SemaphoreType.DMA((2, n))


def reduce_rows(sums, scale):
    n = lax.axis_size("dst")
    width, extent = sums.shape
    return pl.pallas_call(
        functools.partial(rows_kernel, "dst"),
        in_specs=[VMEM] * 2,
        out_specs=VMEM,
        out_shape=jax.ShapeDtypeStruct(sums.shape, jnp.bfloat16),
        scratch_shapes=[
            pltpu.VMEM(sums.shape, jnp.bfloat16),
            pltpu.VMEM((n, width, extent // n), jnp.bfloat16),
            pltpu.VMEM(sums.shape, jnp.bfloat16),
            sem_pairs(n),
            sem_pairs(n),
        ],
        compiler_params=pltpu.CompilerParams(
            collective_id=0, has_side_effects=True, vmem_limit_bytes=LIMIT
        ),
    )(sums, scale)


def reduce_panel(sums, scale, box_total):
    n_src = lax.axis_size("src")
    n_dst = lax.axis_size("dst")
    width, extent = sums.shape
    return pl.pallas_call(
        functools.partial(panel_kernel, box_total),
        in_specs=[VMEM] * 2,
        out_specs=VMEM,
        out_shape=jax.ShapeDtypeStruct(sums.shape, jnp.float32),
        scratch_shapes=[
            pltpu.VMEM(sums.shape, jnp.bfloat16),
            pltpu.VMEM((n_src, width, extent // n_src), jnp.bfloat16),
            pltpu.VMEM(sums.shape, jnp.float32),
            pltpu.VMEM((n_src, width, width), jnp.float32),
            pltpu.VMEM((n_dst, width, width), jnp.float32),
            pltpu.VMEM((n_dst, width, width), jnp.float32),
            sem_pairs(n_src),
            sem_pairs(n_src),
            sem_pairs(n_src),
            sem_pairs(n_dst),
            sem_pairs(n_dst),
        ],
        compiler_params=pltpu.CompilerParams(
            collective_id=1, has_side_effects=True, vmem_limit_bytes=LIMIT
        ),
    )(sums, scale)


def per_device(blocks, block_rows, block_cols, row_counts, col_counts, start_panel):
    rows = row_counts.shape[0]
    cols = col_counts.shape[0]
    box_total = float(cols * lax.axis_size("dst"))
    row_scale = row_counts.reshape(1, rows)
    col_scale = col_counts.reshape(1, cols)
    panel = start_panel
    for _ in range(ITERS):
        u = sweep(1, block_cols, block_rows, panel, col_scale, blocks, rows)
        z = reduce_rows(u, row_scale)
        w = sweep(0, block_rows, block_cols, z, None, blocks, cols)
        panel = reduce_panel(w, col_scale, box_total)
    return panel


def solution(mesh):
    return jax.shard_map(
        per_device,
        mesh=mesh,
        in_specs=(
            P(("groups", "src", "dst"), None, None),
            P(("groups", "src", "dst")),
            P(("groups", "src", "dst")),
            P(("groups", "src")),
            P(("groups", "dst")),
            P(None, ("groups", "dst")),
        ),
        out_specs=P(None, ("groups", "dst")),
        check_vma=False,
    )
```

```python
import functools

import jax
import jax.numpy as jnp
from jax import lax
from jax.experimental import pallas as pl
from jax.experimental.pallas import tpu as pltpu
from jax.sharding import PartitionSpec as P

ITERS = 2
CHUNKS = (64, 32, 16, 8)
MESH = pl.DeviceIdType.MESH
VMEM = pl.BlockSpec(memory_space=pltpu.VMEM)
SMEM = pl.BlockSpec(memory_space=pltpu.SMEM)
LIMIT = 24 * 1024 * 1024


def lanes(index, side):
    return pl.ds(pl.multiple_of(index * side, side), side)


def root_of(counts):
    return jnp.sqrt(counts.astype(jnp.float32))


def sweep_kernel(contract, unroll, gather_ref, scatter_ref, panel_ref, *refs):
    if len(refs) == 6:
        scale_ref, source_ref, out_ref, blocks_ref, sems, scaled = refs
    else:
        source_ref, out_ref, blocks_ref, sems = refs
        scaled = panel_ref
    total, side, _ = blocks_ref.shape

    def fetch(chunk):
        place = pl.ds(chunk * unroll, unroll)
        return pltpu.make_async_copy(source_ref.at[place], blocks_ref.at[place], sems.at[chunk])

    for chunk in range(total // unroll):
        fetch(chunk).start()
    if len(refs) == 6:
        scaled[...] = (panel_ref[...] / root_of(scale_ref[...])).astype(jnp.bfloat16)
    out_ref[...] = jnp.zeros_like(out_ref)

    @pl.loop(0, total // unroll)
    def _(chunk):
        fetch(chunk).wait()
        terms = []
        for k in range(unroll):
            b = chunk * unroll + k
            g = lax.rem(gather_ref[b], scaled.shape[1] // side)
            terms.append(
                lax.dot_general(
                    scaled[:, lanes(g, side)],
                    blocks_ref[b],
                    (((1,), (contract,)), ((), ())),
                    preferred_element_type=jnp.float32,
                )
            )
        for k in range(unroll):
            s = lax.rem(scatter_ref[chunk * unroll + k], out_ref.shape[1] // side)
            out_ref[:, lanes(s, side)] += terms[k]


def sweep(contract, gather_ids, scatter_ids, panel, scale, blocks, out_width):
    unroll = next(c for c in (*CHUNKS, 1) if blocks.shape[0] % c == 0)
    small = [panel] if scale is None else [panel, scale]
    return pl.pallas_call(
        functools.partial(sweep_kernel, contract, unroll),
        in_specs=[SMEM, SMEM, *(VMEM for _ in small), pl.BlockSpec(memory_space=pltpu.HBM)],
        out_specs=VMEM,
        out_shape=jax.ShapeDtypeStruct((panel.shape[0], out_width), jnp.float32),
        scratch_shapes=[
            pltpu.VMEM(blocks.shape, blocks.dtype),
            pltpu.SemaphoreType.DMA((blocks.shape[0] // unroll,)),
            *(pltpu.VMEM(panel.shape, jnp.bfloat16) for _ in small[1:]),
        ],
        compiler_params=pltpu.CompilerParams(vmem_limit_bytes=2 * LIMIT),
    )(gather_ids, scatter_ids, *small, blocks)


def gram(panel):
    return lax.dot_general(
        panel,
        panel,
        (((1,), (1,)), ((), ())),
        precision=lax.Precision.HIGHEST,
        preferred_element_type=jnp.float32,
    )


def inverse_factor(matrix):
    n = matrix.shape[0]
    row = lax.broadcasted_iota(jnp.int32, (n, n), 0)
    col = lax.broadcasted_iota(jnp.int32, (n, n), 1)
    diagonal = row == col
    both = jnp.concatenate([matrix, diagonal.astype(jnp.float32)], axis=1)
    row = lax.broadcasted_iota(jnp.int32, both.shape, 0)
    for j in range(n - 1):
        factor = jnp.broadcast_to(both[:, j : j + 1], both.shape)
        pivot = both[j : j + 1, :] / factor[j : j + 1, :]
        both = both - jnp.where(row > j, factor, 0.0) * pivot
    pivots = jnp.sum(jnp.where(diagonal, both[:, :n], 0.0), axis=1, keepdims=True)
    return both[:, n:] / jnp.sqrt(pivots)


def apply(inverse, panel):
    return jnp.dot(
        inverse, panel, precision=lax.Precision.HIGHEST, preferred_element_type=jnp.float32
    )


def greet(axes):
    barrier = pltpu.get_barrier_semaphore()
    number = 0
    for axis in axes:
        n = lax.axis_size(axis)
        me = lax.axis_index(axis)
        for k in range(1, n):
            pl.semaphore_signal(
                barrier, inc=1, device_id={axis: lax.rem(me + k, n)}, device_id_type=MESH
            )
            number += 1
    pl.semaphore_wait(barrier, number)


def scatter_sums(axis, sums_ref, half, landing, sems):
    n = lax.axis_size(axis)
    me = lax.axis_index(axis)
    part = sums_ref.shape[1] // n
    copies = []
    for k in range(1, n):
        peer = lax.rem(me + k, n)
        copy = pltpu.make_async_remote_copy(
            src_ref=half.at[:, lanes(peer, part)],
            dst_ref=landing.at[k],
            send_sem=sems.at[0, k],
            recv_sem=sems.at[1, k],
            device_id={axis: peer},
            device_id_type=MESH,
        )
        copy.start()
        copies.append(copy)
    mine = lanes(me, part)
    total = sums_ref[:, mine]
    for k in range(1, n):
        copies[k - 1].wait_recv()
        total = total + landing[k].astype(jnp.float32)
    return total, mine, copies


def gather_start(axis, whole, mine, sems):
    n = lax.axis_size(axis)
    me = lax.axis_index(axis)
    copies = []
    for k in range(1, n):
        copy = pltpu.make_async_remote_copy(
            src_ref=whole.at[:, mine],
            dst_ref=whole.at[:, mine],
            send_sem=sems.at[0, k],
            recv_sem=sems.at[1, k],
            device_id={axis: lax.rem(me + k, n)},
            device_id_type=MESH,
        )
        copy.start()
        copies.append(copy)
    return copies


def sum_small(axis, value, slots, sems):
    n = lax.axis_size(axis)
    me = lax.axis_index(axis)
    slots[me] = value
    copies = []
    for k in range(1, n):
        copy = pltpu.make_async_remote_copy(
            src_ref=slots.at[me],
            dst_ref=slots.at[me],
            send_sem=sems.at[0, k],
            recv_sem=sems.at[1, k],
            device_id={axis: lax.rem(me + k, n)},
            device_id_type=MESH,
        )
        copy.start()
        copies.append(copy)
    for copy in copies:
        copy.wait()
    total = slots[0]
    for k in range(1, n):
        total = total + slots[k]
    return total


def rows_kernel(axis, sums_ref, scale_ref, out_ref, half, landing, whole, scatter_sems, gather_sems):
    half[...] = sums_ref[...].astype(jnp.bfloat16)
    greet((axis,))
    total, mine, sent = scatter_sums(axis, sums_ref, half, landing, scatter_sems)
    whole[:, mine] = (total / scale_ref[:, mine].astype(jnp.float32)).astype(jnp.bfloat16)
    gathered = gather_start(axis, whole, mine, gather_sems)
    for copy in sent:
        copy.wait_send()
    for copy in gathered:
        copy.wait()
    out_ref[...] = whole[...]


def panel_kernel(
    box_total,
    sums_ref,
    scale_ref,
    out_ref,
    half,
    landing,
    whole,
    slots_src,
    slots_dst,
    slots_second,
    scatter_sems,
    gather_sems,
    src_sems,
    dst_sems,
    second_sems,
):
    half[...] = sums_ref[...].astype(jnp.bfloat16)
    greet(("src", "dst"))
    total, mine, sent = scatter_sums("src", sums_ref, half, landing, scatter_sems)
    own = (total / root_of(scale_ref[:, mine])).astype(jnp.bfloat16)
    whole[:, mine] = own
    gathered = gather_start("src", whole, mine, gather_sems)
    first = sum_small("src", gram(own.astype(jnp.float32)), slots_src, src_sems)
    first = sum_small("dst", first, slots_dst, dst_sems)
    inverse = inverse_factor(first / box_total)
    for copy in sent:
        copy.wait_send()
    for copy in gathered:
        copy.wait()
    out_ref[...] = apply(inverse, whole[...].astype(jnp.float32))
    second = sum_small("dst", gram(out_ref[...]), slots_second, second_sems)
    out_ref[...] = apply(inverse_factor(second / box_total), out_ref[...])


def sem_pairs(n):
    return pltpu.SemaphoreType.DMA((2, n))


def reduce_rows(sums, scale):
    n = lax.axis_size("dst")
    width, extent = sums.shape
    return pl.pallas_call(
        functools.partial(rows_kernel, "dst"),
        in_specs=[VMEM] * 2,
        out_specs=VMEM,
        out_shape=jax.ShapeDtypeStruct(sums.shape, jnp.bfloat16),
        scratch_shapes=[
            pltpu.VMEM(sums.shape, jnp.bfloat16),
            pltpu.VMEM((n, width, extent // n), jnp.bfloat16),
            pltpu.VMEM(sums.shape, jnp.bfloat16),
            sem_pairs(n),
            sem_pairs(n),
        ],
        compiler_params=pltpu.CompilerParams(
            collective_id=0, has_side_effects=True, vmem_limit_bytes=LIMIT
        ),
    )(sums, scale)


def reduce_panel(sums, scale, box_total):
    n_src = lax.axis_size("src")
    n_dst = lax.axis_size("dst")
    width, extent = sums.shape
    return pl.pallas_call(
        functools.partial(panel_kernel, box_total),
        in_specs=[VMEM] * 2,
        out_specs=VMEM,
        out_shape=jax.ShapeDtypeStruct(sums.shape, jnp.float32),
        scratch_shapes=[
            pltpu.VMEM(sums.shape, jnp.bfloat16),
            pltpu.VMEM((n_src, width, extent // n_src), jnp.bfloat16),
            pltpu.VMEM(sums.shape, jnp.bfloat16),
            pltpu.VMEM((n_src, width, width), jnp.float32),
            pltpu.VMEM((n_dst, width, width), jnp.float32),
            pltpu.VMEM((n_dst, width, width), jnp.float32),
            sem_pairs(n_src),
            sem_pairs(n_src),
            sem_pairs(n_src),
            sem_pairs(n_dst),
            sem_pairs(n_dst),
        ],
        compiler_params=pltpu.CompilerParams(
            collective_id=1, has_side_effects=True, vmem_limit_bytes=LIMIT
        ),
    )(sums, scale)


def per_device(blocks, block_rows, block_cols, row_counts, col_counts, start_panel):
    rows = row_counts.shape[0]
    cols = col_counts.shape[0]
    box_total = float(cols * lax.axis_size("dst"))
    row_scale = row_counts.reshape(1, rows)
    col_scale = col_counts.reshape(1, cols)
    panel = start_panel
    for _ in range(ITERS):
        u = sweep(1, block_cols, block_rows, panel, col_scale, blocks, rows)
        z = reduce_rows(u, row_scale)
        w = sweep(0, block_rows, block_cols, z, None, blocks, cols)
        panel = reduce_panel(w, col_scale, box_total)
    return panel


def solution(mesh):
    return jax.shard_map(
        per_device,
        mesh=mesh,
        in_specs=(
            P(("groups", "src", "dst"), None, None),
            P(("groups", "src", "dst")),
            P(("groups", "src", "dst")),
            P(("groups", "src")),
            P(("groups", "dst")),
            P(None, ("groups", "dst")),
        ),
        out_specs=P(None, ("groups", "dst")),
        check_vma=False,
    )
```

```python
import functools

import jax
import jax.numpy as jnp
from jax import lax
from jax.experimental import pallas as pl
from jax.experimental.pallas import tpu as pltpu
from jax.sharding import PartitionSpec as P

ITERS = 2
CHUNKS = (64, 32, 16, 8)
MESH = pl.DeviceIdType.MESH
VMEM = pl.BlockSpec(memory_space=pltpu.VMEM)
SMEM = pl.BlockSpec(memory_space=pltpu.SMEM)
LIMIT = 24 * 1024 * 1024


def lanes(index, side):
    return pl.ds(pl.multiple_of(index * side, side), side)


def root_of(counts):
    return jnp.sqrt(counts.astype(jnp.float32))


def sweep_kernel(contract, unroll, gather_ref, scatter_ref, panel_ref, *refs):
    if len(refs) == 6:
        scale_ref, source_ref, out_ref, blocks_ref, sems, scaled = refs
    else:
        source_ref, out_ref, blocks_ref, sems = refs
        scaled = panel_ref
    total, side, _ = blocks_ref.shape

    def fetch(chunk):
        place = pl.ds(chunk * unroll, unroll)
        return pltpu.make_async_copy(source_ref.at[place], blocks_ref.at[place], sems.at[chunk])

    for chunk in range(total // unroll):
        fetch(chunk).start()
    if len(refs) == 6:
        scaled[...] = (panel_ref[...] / root_of(scale_ref[...])).astype(jnp.bfloat16)
    out_ref[...] = jnp.zeros_like(out_ref)

    @pl.loop(0, total // unroll)
    def _(chunk):
        fetch(chunk).wait()
        terms = []
        for k in range(unroll):
            b = chunk * unroll + k
            g = lax.rem(gather_ref[b], scaled.shape[1] // side)
            terms.append(
                lax.dot_general(
                    scaled[:, lanes(g, side)],
                    blocks_ref[b],
                    (((1,), (contract,)), ((), ())),
                    preferred_element_type=jnp.float32,
                )
            )
        for k in range(unroll):
            s = lax.rem(scatter_ref[chunk * unroll + k], out_ref.shape[1] // side)
            out_ref[:, lanes(s, side)] += terms[k]


def sweep(contract, gather_ids, scatter_ids, panel, scale, blocks, out_width):
    unroll = next(c for c in (*CHUNKS, 1) if blocks.shape[0] % c == 0)
    small = [panel] if scale is None else [panel, scale]
    return pl.pallas_call(
        functools.partial(sweep_kernel, contract, unroll),
        in_specs=[SMEM, SMEM, *(VMEM for _ in small), pl.BlockSpec(memory_space=pltpu.HBM)],
        out_specs=VMEM,
        out_shape=jax.ShapeDtypeStruct((panel.shape[0], out_width), jnp.float32),
        scratch_shapes=[
            pltpu.VMEM(blocks.shape, blocks.dtype),
            pltpu.SemaphoreType.DMA((blocks.shape[0] // unroll,)),
            *(pltpu.VMEM(panel.shape, jnp.bfloat16) for _ in small[1:]),
        ],
        compiler_params=pltpu.CompilerParams(vmem_limit_bytes=2 * LIMIT),
    )(gather_ids, scatter_ids, *small, blocks)


def gram(panel):
    return lax.dot_general(
        panel,
        panel,
        (((1,), (1,)), ((), ())),
        precision=lax.Precision.HIGHEST,
        preferred_element_type=jnp.float32,
    )


def inverse_factor(matrix):
    n = matrix.shape[0]
    row = lax.broadcasted_iota(jnp.int32, (n, n), 0)
    col = lax.broadcasted_iota(jnp.int32, (n, n), 1)
    diagonal = row == col
    both = jnp.concatenate([matrix, diagonal.astype(jnp.float32)], axis=1)
    row = lax.broadcasted_iota(jnp.int32, both.shape, 0)
    for j in range(n - 1):
        factor = jnp.broadcast_to(both[:, j : j + 1], both.shape)
        pivot = both[j : j + 1, :] / factor[j : j + 1, :]
        both = both - jnp.where(row > j, factor, 0.0) * pivot
    pivots = jnp.sum(jnp.where(diagonal, both[:, :n], 0.0), axis=1, keepdims=True)
    return both[:, n:] / jnp.sqrt(pivots)


def apply(inverse, panel):
    return jnp.dot(
        inverse, panel, precision=lax.Precision.HIGHEST, preferred_element_type=jnp.float32
    )


def greet(axes):
    barrier = pltpu.get_barrier_semaphore()
    number = 0
    for axis in axes:
        n = lax.axis_size(axis)
        me = lax.axis_index(axis)
        for k in range(1, n):
            pl.semaphore_signal(
                barrier, inc=1, device_id={axis: lax.rem(me + k, n)}, device_id_type=MESH
            )
            number += 1
    pl.semaphore_wait(barrier, number)


def scatter_sums(axis, sums_ref, half, landing, sems):
    n = lax.axis_size(axis)
    me = lax.axis_index(axis)
    part = sums_ref.shape[1] // n
    copies = []
    for k in range(1, n):
        peer = lax.rem(me + k, n)
        copy = pltpu.make_async_remote_copy(
            src_ref=half.at[:, lanes(peer, part)],
            dst_ref=landing.at[k],
            send_sem=sems.at[0, k],
            recv_sem=sems.at[1, k],
            device_id={axis: peer},
            device_id_type=MESH,
        )
        copy.start()
        copies.append(copy)
    mine = lanes(me, part)
    total = sums_ref[:, mine]
    for k in range(1, n):
        copies[k - 1].wait_recv()
        total = total + landing[k].astype(jnp.float32)
    return total, mine, copies


def gather_start(axis, whole, mine, sems):
    n = lax.axis_size(axis)
    me = lax.axis_index(axis)
    copies = []
    for k in range(1, n):
        copy = pltpu.make_async_remote_copy(
            src_ref=whole.at[:, mine],
            dst_ref=whole.at[:, mine],
            send_sem=sems.at[0, k],
            recv_sem=sems.at[1, k],
            device_id={axis: lax.rem(me + k, n)},
            device_id_type=MESH,
        )
        copy.start()
        copies.append(copy)
    return copies


def sum_small(axis, value, slots, sems, between=None):
    n = lax.axis_size(axis)
    me = lax.axis_index(axis)
    slots[me] = value
    copies = []
    for k in range(1, n):
        copy = pltpu.make_async_remote_copy(
            src_ref=slots.at[me],
            dst_ref=slots.at[me],
            send_sem=sems.at[0, k],
            recv_sem=sems.at[1, k],
            device_id={axis: lax.rem(me + k, n)},
            device_id_type=MESH,
        )
        copy.start()
        copies.append(copy)
    after = None if between is None else between()
    for copy in copies:
        copy.wait()
    total = slots[0]
    for k in range(1, n):
        total = total + slots[k]
    return total if between is None else (total, after)


def rows_kernel(axis, sums_ref, scale_ref, out_ref, half, landing, whole, scatter_sems, gather_sems):
    half[...] = sums_ref[...].astype(jnp.bfloat16)
    greet((axis,))
    total, mine, sent = scatter_sums(axis, sums_ref, half, landing, scatter_sems)
    whole[:, mine] = (total / scale_ref[:, mine].astype(jnp.float32)).astype(jnp.bfloat16)
    gathered = gather_start(axis, whole, mine, gather_sems)
    for copy in sent:
        copy.wait_send()
    for copy in gathered:
        copy.wait()
    out_ref[...] = whole[...]


def panel_kernel(
    box_total,
    sums_ref,
    scale_ref,
    out_ref,
    half,
    landing,
    whole,
    slots_src,
    slots_dst,
    slots_second,
    scatter_sems,
    gather_sems,
    src_sems,
    dst_sems,
    second_sems,
):
    half[...] = sums_ref[...].astype(jnp.bfloat16)
    greet(("src", "dst"))
    total, mine, sent = scatter_sums("src", sums_ref, half, landing, scatter_sems)
    own = (total / root_of(scale_ref[:, mine])).astype(jnp.bfloat16)
    whole[:, mine] = own
    first, gathered = sum_small(
        "src",
        gram(own.astype(jnp.float32)),
        slots_src,
        src_sems,
        lambda: gather_start("src", whole, mine, gather_sems),
    )
    first = sum_small("dst", first, slots_dst, dst_sems)
    inverse = inverse_factor(first / box_total)
    for copy in sent:
        copy.wait_send()
    for copy in gathered:
        copy.wait()
    out_ref[...] = apply(inverse, whole[...].astype(jnp.float32))
    second = sum_small("dst", gram(out_ref[...]), slots_second, second_sems)
    out_ref[...] = apply(inverse_factor(second / box_total), out_ref[...])


def sem_pairs(n):
    return pltpu.SemaphoreType.DMA((2, n))


def reduce_rows(sums, scale):
    n = lax.axis_size("dst")
    width, extent = sums.shape
    return pl.pallas_call(
        functools.partial(rows_kernel, "dst"),
        in_specs=[VMEM] * 2,
        out_specs=VMEM,
        out_shape=jax.ShapeDtypeStruct(sums.shape, jnp.bfloat16),
        scratch_shapes=[
            pltpu.VMEM(sums.shape, jnp.bfloat16),
            pltpu.VMEM((n, width, extent // n), jnp.bfloat16),
            pltpu.VMEM(sums.shape, jnp.bfloat16),
            sem_pairs(n),
            sem_pairs(n),
        ],
        compiler_params=pltpu.CompilerParams(
            collective_id=0, has_side_effects=True, vmem_limit_bytes=LIMIT
        ),
    )(sums, scale)


def reduce_panel(sums, scale, box_total):
    n_src = lax.axis_size("src")
    n_dst = lax.axis_size("dst")
    width, extent = sums.shape
    return pl.pallas_call(
        functools.partial(panel_kernel, box_total),
        in_specs=[VMEM] * 2,
        out_specs=VMEM,
        out_shape=jax.ShapeDtypeStruct(sums.shape, jnp.float32),
        scratch_shapes=[
            pltpu.VMEM(sums.shape, jnp.bfloat16),
            pltpu.VMEM((n_src, width, extent // n_src), jnp.bfloat16),
            pltpu.VMEM(sums.shape, jnp.bfloat16),
            pltpu.VMEM((n_src, width, width), jnp.float32),
            pltpu.VMEM((n_dst, width, width), jnp.float32),
            pltpu.VMEM((n_dst, width, width), jnp.float32),
            sem_pairs(n_src),
            sem_pairs(n_src),
            sem_pairs(n_src),
            sem_pairs(n_dst),
            sem_pairs(n_dst),
        ],
        compiler_params=pltpu.CompilerParams(
            collective_id=1, has_side_effects=True, vmem_limit_bytes=LIMIT
        ),
    )(sums, scale)


def per_device(blocks, block_rows, block_cols, row_counts, col_counts, start_panel):
    rows = row_counts.shape[0]
    cols = col_counts.shape[0]
    box_total = float(cols * lax.axis_size("dst"))
    row_scale = row_counts.reshape(1, rows)
    col_scale = col_counts.reshape(1, cols)
    panel = start_panel
    for _ in range(ITERS):
        u = sweep(1, block_cols, block_rows, panel, col_scale, blocks, rows)
        z = reduce_rows(u, row_scale)
        w = sweep(0, block_rows, block_cols, z, None, blocks, cols)
        panel = reduce_panel(w, col_scale, box_total)
    return panel


def solution(mesh):
    return jax.shard_map(
        per_device,
        mesh=mesh,
        in_specs=(
            P(("groups", "src", "dst"), None, None),
            P(("groups", "src", "dst")),
            P(("groups", "src", "dst")),
            P(("groups", "src")),
            P(("groups", "dst")),
            P(None, ("groups", "dst")),
        ),
        out_specs=P(None, ("groups", "dst")),
        check_vma=False,
    )
```
